1024 devices in a mesh: pipe: 16 (over x, z_hi), dp: 8 (over z_lo), tensor: 8 (over y, core).
Axes of the slice: x: 4, y: 4, z: 32 (z_hi: 4, z_lo: 8; z = z_hi * 8 + z_lo), core: 2. Of those that a mesh axis runs over, the one named last changes fastest.
Arguments:
- section_out: bfloat16 [16, 1024, 2048], P('pipe', 'dp'), may hold values from -6 to 6
- section_grad: bfloat16 [16, 1024, 2048], P('pipe', 'dp'), may hold values from -6 to 6
- hosted: bfloat16 [16, 2, 1024, 2048], P('pipe', None, 'dp'), may hold values from -6 to 6
- send_slot: int32 [16], P('pipe'), may hold values from 0 to 1
- gain: float32 [16, 2048], P('pipe'), may hold values from 0.5 to 1.5
- w_up: bfloat16 [16, 2048, 6144], P('pipe', None, 'tensor'), may hold values from -0.125 to 0.125
- w_down: bfloat16 [16, 6144, 2048], P('pipe', 'tensor'), may hold values from -0.078125 to 0.078125
Outputs:
- next_forward: bfloat16 [16, 1024, 2048], P('pipe', 'dp')
- next_backward: bfloat16 [16, 1024, 2048], P('pipe', 'dp')
- to_host: bfloat16 [16, 1024, 2048], P('pipe', 'dp')
- gain_grad: float32 [16, 2048], P('pipe')
The draws below stay inside these ranges and needn't reach their ends.
All inputs are finite; a program needn't handle non-finite values.
Results may differ from the reference program's by a relative error of at most 0.015.
Values may be sent and summed in bfloat16 or wider, within the bound.
A program may use at most 64 MiB of HBM per device.

```python
import jax
import jax.numpy as jnp
from jax import lax

D = 2048
FF = 6144
SLOTS = 2
TOKENS = 1024
SECTIONS = 16
N_TENSOR = 8


def set_ends(result, rng, low, largest):
    extent = result.shape
    place = [jax.random.randint(jax.random.fold_in(rng, axis), (), 0, extent[axis]) for axis in range(len(extent))]
    result = result.at[tuple(place)].set(low)
    longest = extent.index(max(extent))
    place[longest] = (place[longest] + 1) % extent[longest]
    return result.at[tuple(place)].set(largest)


def shard_levels(own_key, extent, split, low, high):
    def one(axis_at, blocks):
        heights = jax.random.uniform(jax.random.fold_in(jax.random.fold_in(own_key, 6), axis_at), (blocks,), jnp.float32, low / len(split), high / len(split))
        return jnp.repeat(jnp.exp(heights), extent[axis_at] // blocks).reshape((-1,) + (1,) * (len(extent) - axis_at - 1))

    level = one(*split[0])
    for cut in split[1:]:
        level = level * one(*cut)
    return level


def scatter_about(own_key, extent, width, limit, split=(), kind=jnp.bfloat16):
    level = shard_levels(own_key, extent, split, -0.22, 0.18) if split else 1.0
    drawn = jax.random.normal(own_key, extent, jnp.float32) * width * level
    return jnp.minimum(jnp.maximum(drawn, -limit), limit).astype(kind)


def setup_inputs(seed: int = 0) -> dict:
    key_of = jax.random.split(jax.random.key(seed), 8)
    return {
        "section_out": scatter_about(key_of[0], (SECTIONS, TOKENS, D), 1.0, 6.0, ((0, 16), (1, 8))),
        "section_grad": scatter_about(key_of[1], (SECTIONS, TOKENS, D), 1.0, 6.0, ((0, 16), (1, 8))),
        "hosted": scatter_about(key_of[2], (SECTIONS, SLOTS, TOKENS, D), 1.0, 6.0, ((0, 16), (2, 8))),
        "send_slot": set_ends(jax.random.randint(key_of[3], (SECTIONS,), 0, SLOTS), jax.random.fold_in(key_of[3], 1), 0, SLOTS - 1).astype(jnp.int32),
        "gain": jnp.clip(0.5 + 1.0 * jax.random.uniform(key_of[4], (SECTIONS, D), jnp.float32) ** shard_levels(key_of[4], (SECTIONS, D), ((0, 16),), -0.2, 0.2), 0.5, 1.5),
        "w_up": scatter_about(key_of[5], (SECTIONS, D, FF), D ** -0.5, 0.125, ((0, 16), (2, 8))),
        "w_down": scatter_about(key_of[6], (SECTIONS, FF, D), FF ** -0.5, 0.078125, ((0, 16), (1, 8))),
    }


epsilon = 1e-05

def normalize(activation):
    values = activation.astype(jnp.float32)
    factor = lax.rsqrt(lax.optimization_barrier(jnp.mean(values * values, axis=-1, keepdims=True)) + epsilon)
    return (values * factor, factor)

def shard_sum(left, right):
    blocked_left = left.astype(jnp.float32).reshape(left.shape[0], N_TENSOR, -1)
    blocked_right = right.astype(jnp.float32).reshape(N_TENSOR, -1, right.shape[1])
    partial_sums = jnp.einsum('tkf,kfd->ktd', blocked_left, blocked_right)
    rounded = lax.optimization_barrier(partial_sums.astype(jnp.bfloat16))
    return lax.optimization_barrier(jnp.sum(rounded.astype(jnp.float32), axis=0))

def silu_slope(pre):
    sigma = jax.nn.sigmoid(pre)
    return sigma * (1.0 + pre * (1.0 - sigma))

def one_section(operands):
    forward_in, incoming, saved, gains, weights_up, weights_down = operands
    forward_hat = normalize(forward_in)[0]
    normed = (forward_hat * gains).astype(jnp.bfloat16)
    hidden = jax.nn.silu(jnp.dot(normed, weights_up, preferred_element_type=jnp.float32)).astype(jnp.bfloat16)
    mixed = shard_sum(hidden, weights_down)
    next_forward = (forward_in.astype(jnp.float32) + mixed).astype(jnp.bfloat16)
    saved_hat, saved_factor = normalize(saved)
    saved_normed = (saved_hat * gains).astype(jnp.bfloat16)
    saved_pre = jnp.dot(saved_normed, weights_up, preferred_element_type=jnp.float32)
    hidden_grad = jnp.dot(incoming, weights_down.T, preferred_element_type=jnp.float32)
    pre_grad = (hidden_grad * silu_slope(saved_pre)).astype(jnp.bfloat16)
    normed_grad = shard_sum(pre_grad, weights_up.T)
    hat_grad = normed_grad * gains
    input_grad = saved_factor * (hat_grad - saved_hat * lax.optimization_barrier(jnp.mean(hat_grad * saved_hat, axis=-1, keepdims=True)))
    next_backward = (incoming.astype(jnp.float32) + input_grad).astype(jnp.bfloat16)
    gain_grad = lax.optimization_barrier(jnp.sum(normed_grad * saved_hat, axis=0))
    return (next_forward, next_backward, gain_grad)

def reference(section_out, section_grad, hosted, send_slot, gain, w_up, w_down):
    forward_in = jnp.roll(section_out, 1, axis=0)
    incoming = jnp.roll(section_grad, -1, axis=0)
    slot_index = send_slot.astype(jnp.int32)[:, None, None, None]
    chosen = jnp.take_along_axis(hosted, slot_index, axis=1)[:, 0]
    saved = chosen[::-1]
    to_host = forward_in[::-1]
    next_forward, next_backward, gain_grad = lax.map(one_section, (forward_in, incoming, saved, gain, w_up, w_down))
    return (next_forward, next_backward, to_host, gain_grad)
```

```python
import functools

import jax
import jax.numpy as jnp
from jax import lax
from jax.experimental import pallas as pl
from jax.experimental.pallas import tpu as pltpu
from jax.sharding import PartitionSpec as P

epsilon = 1e-05
MESH = pl.DeviceIdType.MESH
F32, BF16 = jnp.float32, jnp.bfloat16
TILE = 256


def remote(src, dst, send, recv, **where):
    return pltpu.make_async_remote_copy(
        src_ref=src, dst_ref=dst, send_sem=send, recv_sem=recv, device_id=where, device_id_type=MESH
    )


def rms(values):
    factor = lax.rsqrt(jnp.mean(values * values, axis=-1, keepdims=True) + epsilon)
    return values * factor, factor


def kernel(
    n_pipe, n_dp, n_tensor,
    slot_ref, out_in, grad_in, host_in, gain_ref, up_in, down_in,
    nf_out, nb_out, th_out, gg_out,
    up, down, both, chosen, fwd_own, sav_own, hat_own,
    norm_f, norm_s, inc, part_f, part_b, sum_f, sum_b, end_f, end_b,
    mid, gain_own, gain_dp, gain_mid, gain_tp,
    local_sem, z_send, z_recv, ag_send, ag_recv, rs_send, rs_recv, gd_send, gd_recv, gt_send, gt_recv,
):
    s, d, t = lax.axis_index("pipe"), lax.axis_index("dp"), lax.axis_index("tensor")
    rows = out_in.shape[1] // n_tensor
    width, hidden_units = up.shape
    core = t % 2
    sibling = t + 1 - 2 * core
    across = [(t + 2 * p) % n_tensor for p in range(1, n_tensor // 2)]
    peers = [(t + p) % n_tensor for p in range(1, n_tensor)]
    dp_peers = [(d + p) % n_dp for p in range(1, n_dp)]
    after, before = (s + 1) % n_pipe, (s + n_pipe - 1) % n_pipe
    mirror, keeper = n_pipe - 1 - s, (2 * n_pipe - 2 - s) % n_pipe
    own = pl.ds(pl.multiple_of(t * rows, rows), rows)

    def chunk(ref, k):
        return ref.at[0, pl.ds(pl.multiple_of(k * rows, rows), rows)]

    load_host = pltpu.make_async_copy(host_in.at[0, :, own], both, local_sem.at[0])
    load_host.start()
    load_up = pltpu.make_async_copy(up_in.at[0], up, local_sem.at[1])
    load_up.start()
    load_down = pltpu.make_async_copy(down_in.at[0], down, local_sem.at[2])
    load_down.start()

    barrier = pltpu.get_barrier_semaphore()
    for where in [{"pipe": after}, {"pipe": before}, {"pipe": mirror}]:
        pl.semaphore_signal(barrier, inc=1, device_id=where, device_id_type=MESH)

    @pl.when(keeper != s)
    def _():
        pl.semaphore_signal(barrier, inc=1, device_id={"pipe": keeper}, device_id_type=MESH)

    for k in dp_peers:
        pl.semaphore_signal(barrier, inc=1, device_id={"dp": k}, device_id_type=MESH)
    for k in peers:
        pl.semaphore_signal(barrier, inc=1, device_id={"tensor": k}, device_id_type=MESH)
    load_host.wait()
    chosen[...] = both[slot_ref[0]]
    pl.semaphore_wait(barrier, 3 + len(dp_peers) + len(peers) + jnp.where(keeper != s, 1, 0))

    z_s = remote(chosen, sav_own, z_send.at[0], z_recv.at[0], pipe=mirror)
    z_g = remote(grad_in.at[0, own], inc.at[t], z_send.at[1], z_recv.at[1], pipe=before)
    z_f = remote(out_in.at[0, own], fwd_own, z_send.at[2], z_recv.at[2], pipe=after)
    z_t = remote(out_in.at[0, own], chunk(th_out, t), z_send.at[3], z_recv.at[3], pipe=keeper)
    l_t = pltpu.make_async_copy(out_in.at[0, own], chunk(th_out, t), local_sem.at[3])
    z_s.start()
    z_g.start()
    z_f.start()

    def gather_start(which, at):
        for i, k in enumerate([sibling] + across):
            remote(at(t), at(t), ag_send.at[which, i], ag_recv.at[which, t], tensor=k).start()

    def gather_pass(which, at):
        for i, k in enumerate(across):
            remote(at(k), at(k), ag_send.at[which, 4 + i], ag_recv.at[which, k], tensor=k).wait_recv()
            remote(at(k), at(k), ag_send.at[which, 4 + i], ag_recv.at[which, k], tensor=sibling).start()

    def gather_wait(which, at):
        for k in [sibling] + [k + 1 - 2 * core for k in across]:
            remote(at(k), at(k), ag_send.at[which, 0], ag_recv.at[which, k], tensor=sibling).wait_recv()

    def gather_sent(which, at):
        for i, k in enumerate([sibling] + across):
            remote(at(t), at(t), ag_send.at[which, i], ag_recv.at[which, t], tensor=k).wait_send()
        for i, k in enumerate(across):
            remote(at(k), at(k), ag_send.at[which, 4 + i], ag_recv.at[which, k], tensor=sibling).wait_send()

    at_s, at_g, at_f = (lambda k: norm_s.at[k]), (lambda k: inc.at[k]), (lambda k: norm_f.at[k])
    at_t, at_nb, at_nf = (
        functools.partial(chunk, th_out), functools.partial(chunk, nb_out), functools.partial(chunk, nf_out)
    )
    gains = gain_ref[...]

    z_s.wait_recv()
    hat, saved_factor = rms(sav_own[...].astype(F32))
    hat_own[...] = hat
    norm_s[t] = (hat * gains).astype(BF16)
    gather_start(0, at_s)
    z_g.wait_recv()
    gather_start(1, at_g)
    z_f.wait_recv()
    norm_f[t] = (rms(fwd_own[...].astype(F32))[0] * gains).astype(BF16)
    gather_start(2, at_f)

    @pl.when(keeper != s)
    def _():
        z_t.start()

    @pl.when(keeper == s)
    def _():
        l_t.start()

    gather_pass(0, at_s)
    gather_pass(1, at_g)
    gather_pass(2, at_f)
    gather_wait(0, at_s)
    gather_wait(1, at_g)

    tokens = n_tensor * rows
    nt = (((1,), (1,)), ((), ()))

    def cut(i):
        return pl.ds(pl.multiple_of(i * TILE, TILE), TILE)

    load_up.wait()
    load_down.wait()

    @pl.loop(0, hidden_units // TILE)
    def _(i):
        pre = jnp.dot(norm_s[...].reshape(tokens, width), up[:, cut(i)], preferred_element_type=F32)
        back = lax.dot_general(inc[...].reshape(tokens, width), down[cut(i), :], nt, preferred_element_type=F32)
        sigma = jax.nn.sigmoid(pre)
        mid[0, :, cut(i)] = (back * (sigma * (1.0 + pre * (1.0 - sigma)))).astype(BF16)

    @pl.loop(0, width // TILE)
    def _(i):
        part = lax.dot_general(mid[0], up[cut(i), :], nt, preferred_element_type=F32)
        part_b[:, :, cut(i)] = part.astype(BF16).reshape(n_tensor, rows, TILE)

    def scatter_start(which, part, total):
        for i, k in enumerate(peers):
            remote(part.at[k], total.at[t], rs_send.at[which, i], rs_recv.at[which, t], tensor=k).start()

    def scatter_sum(which, part, total):
        acc = part[t].astype(F32)
        for i, k in enumerate(peers):
            remote(part.at[k], total.at[k], rs_send.at[which, i], rs_recv.at[which, k], tensor=k).wait_recv()
            acc += total[k].astype(F32)
        return acc

    def scatter_sent(which, part, total):
        for i, k in enumerate(peers):
            remote(part.at[k], total.at[t], rs_send.at[which, i], rs_recv.at[which, t], tensor=k).wait_send()

    scatter_start(0, part_b, sum_b)
    gather_wait(2, at_f)

    @pl.loop(0, hidden_units // TILE)
    def _(i):
        pre = jnp.dot(norm_f[...].reshape(tokens, width), up[:, cut(i)], preferred_element_type=F32)
        mid[1, :, cut(i)] = jax.nn.silu(pre).astype(BF16)

    @pl.loop(0, width // TILE)
    def _(i):
        part = jnp.dot(mid[1], down[:, cut(i)], preferred_element_type=F32)
        part_f[:, :, cut(i)] = part.astype(BF16).reshape(n_tensor, rows, TILE)

    scatter_start(1, part_f, sum_f)

    normed_grad = scatter_sum(0, part_b, sum_b)
    hat = hat_own[...]
    gain_own[...] = jnp.sum(normed_grad * hat, axis=0, keepdims=True)
    for i, k in enumerate(dp_peers):
        remote(gain_own, gain_dp.at[d], gd_send.at[i], gd_recv.at[d], dp=k).start()
    hat_grad = normed_grad * gains
    input_grad = saved_factor * (hat_grad - hat * jnp.mean(hat_grad * hat, axis=-1, keepdims=True))
    end_b[...] = (inc[t].astype(F32) + input_grad).astype(BF16)

    def ends_start(which, end, at):
        keep = pltpu.make_async_copy(end, at(t), local_sem.at[which])
        keep.start()
        for i, k in enumerate([sibling] + across):
            remote(end, at(t), ag_send.at[which, i], ag_recv.at[which, t], tensor=k).start()
        return keep

    keep_b = ends_start(4, end_b, at_nb)
    mixed = scatter_sum(1, part_f, sum_f)
    end_f[...] = (fwd_own[...].astype(F32) + mixed).astype(BF16)
    keep_f = ends_start(5, end_f, at_nf)

    @pl.when(keeper != s)
    def _():
        z_t.wait()

    @pl.when(keeper == s)
    def _():
        l_t.wait()

    gather_start(3, at_t)

    acc = gain_own[...]
    for i, k in enumerate(dp_peers):
        remote(gain_own, gain_dp.at[k], gd_send.at[i], gd_recv.at[k], dp=k).wait_recv()
        acc += gain_dp[k]
    gain_mid[...] = acc
    for i, k in enumerate(peers):
        remote(gain_mid, gain_tp.at[t], gt_send.at[i], gt_recv.at[t], tensor=k).start()

    gather_pass(4, at_nb)
    gather_pass(5, at_nf)
    gather_pass(3, at_t)

    for i, k in enumerate(peers):
        remote(gain_mid, gain_tp.at[k], gt_send.at[i], gt_recv.at[k], tensor=k).wait_recv()
        acc += gain_tp[k]
    gg_out[...] = acc

    gather_wait(4, at_nb)
    gather_wait(5, at_nf)
    gather_wait(3, at_t)
    keep_b.wait()
    keep_f.wait()
    z_s.wait_send()
    z_g.wait_send()
    z_f.wait_send()
    for which, at in enumerate((at_s, at_g, at_f, at_t, at_nb, at_nf)):
        gather_sent(which, at)
    scatter_sent(0, part_b, sum_b)
    scatter_sent(1, part_f, sum_f)
    for i, k in enumerate(dp_peers):
        remote(gain_own, gain_dp.at[d], gd_send.at[i], gd_recv.at[d], dp=k).wait_send()
    for i, k in enumerate(peers):
        remote(gain_mid, gain_tp.at[t], gt_send.at[i], gt_recv.at[t], tensor=k).wait_send()


def body(section_out, section_grad, hosted, send_slot, gain, w_up, w_down):
    n_pipe, n_dp, n_tensor = (lax.axis_size(a) for a in ("pipe", "dp", "tensor"))
    _, tokens, width = section_out.shape
    units = w_up.shape[2]
    rows = tokens // n_tensor
    dma = pltpu.SemaphoreType.DMA
    whole = jax.ShapeDtypeStruct(section_out.shape, BF16)
    anywhere = pl.BlockSpec(memory_space=pl.ANY)
    in_vmem = pl.BlockSpec(memory_space=pltpu.VMEM)
    gathered = pltpu.VMEM((n_tensor, rows, width), BF16)
    row_block = pltpu.VMEM((rows, width), BF16)
    gain_row = pltpu.VMEM((1, width), F32)
    return pl.pallas_call(
        functools.partial(kernel, n_pipe, n_dp, n_tensor),
        out_shape=(whole, whole, whole, jax.ShapeDtypeStruct((1, width), F32)),
        in_specs=[
            pl.BlockSpec(memory_space=pltpu.SMEM), anywhere, anywhere, anywhere, in_vmem, anywhere, anywhere,
        ],
        out_specs=(anywhere, anywhere, anywhere, in_vmem),
        scratch_shapes=[
            pltpu.VMEM((width, units), BF16), pltpu.VMEM((units, width), BF16),
            pltpu.VMEM((hosted.shape[1], rows, width), BF16), row_block, row_block, row_block,
            pltpu.VMEM((rows, width), F32),
            gathered, gathered, gathered, gathered, gathered, gathered, gathered, row_block, row_block,
            pltpu.VMEM((2, tokens, units), BF16),
            gain_row, pltpu.VMEM((n_dp, 1, width), F32), gain_row, pltpu.VMEM((n_tensor, 1, width), F32),
            dma((6,)), dma((4,)), dma((4,)), dma((6, n_tensor)), dma((6, n_tensor)),
            dma((2, n_tensor)), dma((2, n_tensor)), dma((n_dp,)), dma((n_dp,)), dma((n_tensor,)), dma((n_tensor,)),
        ],
        compiler_params=pltpu.CompilerParams(
            collective_id=0, has_side_effects=True, vmem_limit_bytes=50 * 2**20
        ),
    )(send_slot, section_out, section_grad, hosted, gain, w_up, w_down)


def solution(mesh):
    placed = (
        P("pipe", "dp", None),
        P("pipe", "dp", None),
        P("pipe", None, "dp", None),
        P("pipe"),
        P("pipe", None),
        P("pipe", None, "tensor"),
        P("pipe", "tensor", None),
    )
    return jax.shard_map(
        body,
        mesh=mesh,
        in_specs=placed,
        out_specs=(
            P("pipe", "dp", None),
            P("pipe", "dp", None),
            P("pipe", "dp", None),
            P("pipe", None),
        ),
        check_vma=False,
    )
```

```python
import functools

import jax
import jax.numpy as jnp
from jax import lax
from jax.experimental import pallas as pl
from jax.experimental.pallas import tpu as pltpu
from jax.sharding import PartitionSpec as P

epsilon = 1e-05
MESH = pl.DeviceIdType.MESH
F32, BF16 = jnp.float32, jnp.bfloat16
TILE = 256
CUTS = 4


def remote(src, dst, send, recv, **where):
    return pltpu.make_async_remote_copy(
        src_ref=src, dst_ref=dst, send_sem=send, recv_sem=recv, device_id=where, device_id_type=MESH
    )


def rms(values):
    factor = lax.rsqrt(jnp.mean(values * values, axis=-1, keepdims=True) + epsilon)
    return values * factor, factor


def kernel(
    n_pipe, n_dp, n_tensor,
    slot_ref, out_in, grad_in, host_in, gain_ref, up_in, down_in,
    nf_out, nb_out, th_out, gg_out,
    up, down, both, chosen, fwd_own, sav_own, hat_own,
    norm_f, norm_s, inc, part_f, part_b, sum_f, sum_b, end_f, end_b,
    mid, pair, gain_own, gain_dp, gain_mid, gain_tp,
    local_sem, z_send, z_recv, ag_send, ag_recv, rs_send, rs_recv, pr_send, pr_recv, gd_send, gd_recv, gt_send, gt_recv,
):
    s, d, t = lax.axis_index("pipe"), lax.axis_index("dp"), lax.axis_index("tensor")
    rows = out_in.shape[1] // n_tensor
    width, hidden_units = up.shape
    core = t % 2
    sibling = t + 1 - 2 * core
    across = [(t + 2 * p) % n_tensor for p in range(1, n_tensor // 2)]
    peers = [(t + p) % n_tensor for p in range(1, n_tensor)]
    dp_peers = [(d + p) % n_dp for p in range(1, n_dp)]
    after, before = (s + 1) % n_pipe, (s + n_pipe - 1) % n_pipe
    mirror, keeper = n_pipe - 1 - s, (2 * n_pipe - 2 - s) % n_pipe
    own = pl.ds(pl.multiple_of(t * rows, rows), rows)

    def chunk(ref, k):
        return ref.at[0, pl.ds(pl.multiple_of(k * rows, rows), rows)]

    load_host = pltpu.make_async_copy(host_in.at[0, :, own], both, local_sem.at[0])
    load_host.start()
    load_up = pltpu.make_async_copy(up_in.at[0], up, local_sem.at[1])
    load_up.start()
    load_down = pltpu.make_async_copy(down_in.at[0], down, local_sem.at[2])
    load_down.start()

    barrier = pltpu.get_barrier_semaphore()
    for where in [{"pipe": after}, {"pipe": before}, {"pipe": mirror}]:
        pl.semaphore_signal(barrier, inc=1, device_id=where, device_id_type=MESH)

    @pl.when(keeper != s)
    def _():
        pl.semaphore_signal(barrier, inc=1, device_id={"pipe": keeper}, device_id_type=MESH)

    for k in dp_peers:
        pl.semaphore_signal(barrier, inc=1, device_id={"dp": k}, device_id_type=MESH)
    for k in peers:
        pl.semaphore_signal(barrier, inc=1, device_id={"tensor": k}, device_id_type=MESH)
    load_host.wait()
    chosen[...] = both[slot_ref[0]]
    pl.semaphore_wait(barrier, 3 + len(dp_peers) + len(peers) + jnp.where(keeper != s, 1, 0))

    z_s = remote(chosen, sav_own, z_send.at[0], z_recv.at[0], pipe=mirror)
    z_g = remote(grad_in.at[0, own], inc.at[t], z_send.at[1], z_recv.at[1], pipe=before)
    z_f = remote(out_in.at[0, own], fwd_own, z_send.at[2], z_recv.at[2], pipe=after)
    z_t = remote(out_in.at[0, own], chunk(th_out, t), z_send.at[3], z_recv.at[3], pipe=keeper)
    l_t = pltpu.make_async_copy(out_in.at[0, own], chunk(th_out, t), local_sem.at[3])
    z_s.start()
    z_g.start()
    z_f.start()

    def gather_start(which, at):
        for i, k in enumerate([sibling] + across):
            remote(at(t), at(t), ag_send.at[which, i], ag_recv.at[which, t], tensor=k).start()

    def gather_pass(which, at):
        for i, k in enumerate(across):
            remote(at(k), at(k), ag_send.at[which, 4 + i], ag_recv.at[which, k], tensor=k).wait_recv()
            remote(at(k), at(k), ag_send.at[which, 4 + i], ag_recv.at[which, k], tensor=sibling).start()

    def gather_wait(which, at):
        for k in [sibling] + [k + 1 - 2 * core for k in across]:
            remote(at(k), at(k), ag_send.at[which, 0], ag_recv.at[which, k], tensor=sibling).wait_recv()

    def gather_sent(which, at):
        for i, k in enumerate([sibling] + across):
            remote(at(t), at(t), ag_send.at[which, i], ag_recv.at[which, t], tensor=k).wait_send()
        for i, k in enumerate(across):
            remote(at(k), at(k), ag_send.at[which, 4 + i], ag_recv.at[which, k], tensor=sibling).wait_send()

    at_s, at_g, at_f = (lambda k: norm_s.at[k]), (lambda k: inc.at[k]), (lambda k: norm_f.at[k])
    at_t, at_nb, at_nf = (
        functools.partial(chunk, th_out), functools.partial(chunk, nb_out), functools.partial(chunk, nf_out)
    )
    gains = gain_ref[...]

    z_s.wait_recv()
    hat, saved_factor = rms(sav_own[...].astype(F32))
    hat_own[...] = hat
    norm_s[t] = (hat * gains).astype(BF16)
    gather_start(0, at_s)
    z_g.wait_recv()
    gather_start(1, at_g)
    z_f.wait_recv()
    norm_f[t] = (rms(fwd_own[...].astype(F32))[0] * gains).astype(BF16)
    gather_start(2, at_f)

    @pl.when(keeper != s)
    def _():
        z_t.start()

    @pl.when(keeper == s)
    def _():
        l_t.start()

    gather_pass(0, at_s)
    gather_pass(1, at_g)
    gather_pass(2, at_f)
    gather_wait(0, at_s)
    gather_wait(1, at_g)

    tokens = n_tensor * rows
    nt = (((1,), (1,)), ((), ()))

    def cut(i):
        return pl.ds(pl.multiple_of(i * TILE, TILE), TILE)

    load_up.wait()
    load_down.wait()

    @pl.loop(0, hidden_units // TILE)
    def _(i):
        pre = jnp.dot(norm_s[...].reshape(tokens, width), up[:, cut(i)], preferred_element_type=F32)
        back = lax.dot_general(inc[...].reshape(tokens, width), down[cut(i), :], nt, preferred_element_type=F32)
        sigma = jax.nn.sigmoid(pre)
        mid[0, :, cut(i)] = (back * (sigma * (1.0 + pre * (1.0 - sigma)))).astype(BF16)

    @pl.loop(0, width // TILE)
    def _(i):
        part = lax.dot_general(mid[0], up[cut(i), :], nt, preferred_element_type=F32)
        part_b[:, :, cut(i)] = part.astype(BF16).reshape(n_tensor, rows, TILE)

    y_own, y_all = t // 2, n_tensor // 2
    far = [(y_own + p) % y_all for p in sorted(range(1, y_all), key=lambda p: -min(p, y_all - p))]

    def pair_copy(which, part, y):
        k = 2 * y + 1 - core
        return remote(part.at[k], pair.at[which, y], pr_send.at[which, y], pr_recv.at[which, y], tensor=sibling)

    def pair_sum(which, part, y):
        pair_copy(which, part, y).wait_recv()
        return part[2 * y + core].astype(F32) + pair[which, y].astype(F32)

    def scatter_start(which, part, total):
        for y in far + [y_own]:
            pair_copy(which, part, y).start()
        for i, y in enumerate(far):
            k = 2 * y + core
            part[k] = pair_sum(which, part, y).astype(BF16)
            remote(part.at[k], total.at[y_own], rs_send.at[which, i], rs_recv.at[which, y_own], tensor=k).start()

    def scatter_sum(which, part, total):
        acc = pair_sum(which, part, y_own)
        for i, y in enumerate(far):
            k = 2 * y + core
            remote(part.at[k], total.at[y], rs_send.at[which, i], rs_recv.at[which, y], tensor=k).wait_recv()
            acc += total[y].astype(F32)
        return acc

    def scatter_sent(which, part, total):
        for y in far + [y_own]:
            pair_copy(which, part, y).wait_send()
        for i, y in enumerate(far):
            k = 2 * y + core
            remote(part.at[k], total.at[y_own], rs_send.at[which, i], rs_recv.at[which, y_own], tensor=k).wait_send()

    scatter_start(0, part_b, sum_b)
    gather_wait(2, at_f)

    @pl.loop(0, hidden_units // TILE)
    def _(i):
        pre = jnp.dot(norm_f[...].reshape(tokens, width), up[:, cut(i)], preferred_element_type=F32)
        mid[1, :, cut(i)] = jax.nn.silu(pre).astype(BF16)

    @pl.loop(0, width // TILE)
    def _(i):
        part = jnp.dot(mid[1], down[:, cut(i)], preferred_element_type=F32)
        part_f[:, :, cut(i)] = part.astype(BF16).reshape(n_tensor, rows, TILE)

    scatter_start(1, part_f, sum_f)

    normed_grad = scatter_sum(0, part_b, sum_b)
    hat = hat_own[...]
    gain_own[...] = jnp.sum(normed_grad * hat, axis=0, keepdims=True)
    for i, k in enumerate(dp_peers):
        remote(gain_own, gain_dp.at[d], gd_send.at[i], gd_recv.at[d], dp=k).start()
    hat_grad = normed_grad * gains
    input_grad = saved_factor * (hat_grad - hat * jnp.mean(hat_grad * hat, axis=-1, keepdims=True))
    end_b[...] = (inc[t].astype(F32) + input_grad).astype(BF16)

    def ends_start(which, end, at):
        keep = pltpu.make_async_copy(end, at(t), local_sem.at[which])
        keep.start()
        for i, k in enumerate([sibling] + across):
            remote(end, at(t), ag_send.at[which, i], ag_recv.at[which, t], tensor=k).start()
        return keep

    keep_b = ends_start(4, end_b, at_nb)
    mixed = scatter_sum(1, part_f, sum_f)
    end_f[...] = (fwd_own[...].astype(F32) + mixed).astype(BF16)
    keep_f = ends_start(5, end_f, at_nf)

    @pl.when(keeper != s)
    def _():
        z_t.wait()

    @pl.when(keeper == s)
    def _():
        l_t.wait()

    gather_start(3, at_t)

    acc = gain_own[...]
    for i, k in enumerate(dp_peers):
        remote(gain_own, gain_dp.at[k], gd_send.at[i], gd_recv.at[k], dp=k).wait_recv()
        acc += gain_dp[k]
    gain_mid[...] = acc
    for i, k in enumerate(peers):
        remote(gain_mid, gain_tp.at[t], gt_send.at[i], gt_recv.at[t], tensor=k).start()

    gather_pass(4, at_nb)
    gather_pass(5, at_nf)
    gather_pass(3, at_t)

    for i, k in enumerate(peers):
        remote(gain_mid, gain_tp.at[k], gt_send.at[i], gt_recv.at[k], tensor=k).wait_recv()
        acc += gain_tp[k]
    gg_out[...] = acc

    gather_wait(4, at_nb)
    gather_wait(5, at_nf)
    gather_wait(3, at_t)
    keep_b.wait()
    keep_f.wait()
    z_s.wait_send()
    z_g.wait_send()
    z_f.wait_send()
    for which, at in enumerate((at_s, at_g, at_f, at_t, at_nb, at_nf)):
        gather_sent(which, at)
    scatter_sent(0, part_b, sum_b)
    scatter_sent(1, part_f, sum_f)
    for i, k in enumerate(dp_peers):
        remote(gain_own, gain_dp.at[d], gd_send.at[i], gd_recv.at[d], dp=k).wait_send()
    for i, k in enumerate(peers):
        remote(gain_mid, gain_tp.at[t], gt_send.at[i], gt_recv.at[t], tensor=k).wait_send()


def move_out(*refs):
    sources, ends, held, gain_held, sems, gain_sem = refs[:4], refs[4:8], *refs[8:]
    rows = sources[0].shape[1] // CUTS
    steps = [(sources[3], gain_held, ends[3], gain_sem)]
    for i in range(3):
        for j in range(CUTS):
            part = pl.ds(j * rows, rows)
            steps.append((sources[i].at[0, part], held.at[i, part], ends[i].at[0, part], sems.at[i, j]))
    for source, spot, _, sem in steps:
        pltpu.make_async_copy(source, spot, sem).start()
    for source, spot, end, sem in steps:
        pltpu.make_async_copy(source, spot, sem).wait()
        pltpu.make_async_copy(spot, end, sem).start()
    for _, spot, end, sem in steps:
        pltpu.make_async_copy(spot, end, sem).wait()


def body(section_out, section_grad, hosted, send_slot, gain, w_up, w_down):
    n_pipe, n_dp, n_tensor = (lax.axis_size(a) for a in ("pipe", "dp", "tensor"))
    _, tokens, width = section_out.shape
    units = w_up.shape[2]
    rows = tokens // n_tensor
    dma = pltpu.SemaphoreType.DMA
    whole = jax.ShapeDtypeStruct(section_out.shape, BF16)
    anywhere = pl.BlockSpec(memory_space=pl.ANY)
    in_vmem = pl.BlockSpec(memory_space=pltpu.VMEM)
    gathered = pltpu.VMEM((n_tensor, rows, width), BF16)
    row_block = pltpu.VMEM((rows, width), BF16)
    gain_row = pltpu.VMEM((1, width), F32)
    results = pl.pallas_call(
        functools.partial(kernel, n_pipe, n_dp, n_tensor),
        out_shape=(whole, whole, whole, jax.ShapeDtypeStruct((1, width), F32)),
        in_specs=[
            pl.BlockSpec(memory_space=pltpu.SMEM), anywhere, anywhere, anywhere, in_vmem, anywhere, anywhere,
        ],
        out_specs=(anywhere, anywhere, anywhere, in_vmem),
        scratch_shapes=[
            pltpu.VMEM((width, units), BF16), pltpu.VMEM((units, width), BF16),
            pltpu.VMEM((hosted.shape[1], rows, width), BF16), row_block, row_block, row_block,
            pltpu.VMEM((rows, width), F32),
            gathered, gathered, gathered, gathered, gathered, gathered, gathered, row_block, row_block,
            pltpu.VMEM((2, tokens, units), BF16), pltpu.VMEM((2, n_tensor // 2, rows, width), BF16),
            gain_row, pltpu.VMEM((n_dp, 1, width), F32), gain_row, pltpu.VMEM((n_tensor, 1, width), F32),
            dma((6,)), dma((4,)), dma((4,)), dma((6, n_tensor)), dma((6, n_tensor)),
            dma((2, n_tensor)), dma((2, n_tensor)), dma((2, n_tensor)), dma((2, n_tensor)), dma((n_dp,)), dma((n_dp,)), dma((n_tensor,)), dma((n_tensor,)),
        ],
        compiler_params=pltpu.CompilerParams(
            collective_id=0, has_side_effects=True, vmem_limit_bytes=60 * 2**20
        ),
    )(send_slot, section_out, section_grad, hosted, gain, w_up, w_down)
    return pl.pallas_call(
        move_out,
        out_shape=tuple(jax.ShapeDtypeStruct(r.shape, r.dtype) for r in results),
        in_specs=[anywhere] * 4,
        out_specs=(anywhere,) * 4,
        scratch_shapes=[pltpu.VMEM((3, tokens, width), BF16), gain_row, dma((3, CUTS)), dma(())],
        compiler_params=pltpu.CompilerParams(vmem_limit_bytes=60 * 2**20),
    )(*results)


def solution(mesh):
    placed = (
        P("pipe", "dp", None),
        P("pipe", "dp", None),
        P("pipe", None, "dp", None),
        P("pipe"),
        P("pipe", None),
        P("pipe", None, "tensor"),
        P("pipe", "tensor", None),
    )
    return jax.shard_map(
        body,
        mesh=mesh,
        in_specs=placed,
        out_specs=(
            P("pipe", "dp", None),
            P("pipe", "dp", None),
            P("pipe", "dp", None),
            P("pipe", None),
        ),
        check_vma=False,
    )
```

```python
import functools

import jax
import jax.numpy as jnp
from jax import lax
from jax.experimental import pallas as pl
from jax.experimental.pallas import tpu as pltpu
from jax.sharding import PartitionSpec as P

epsilon = 1e-05
MESH = pl.DeviceIdType.MESH
F32, BF16 = jnp.float32, jnp.bfloat16
TILE = 256
CUTS = 4


def remote(src, dst, send, recv, **where):
    return pltpu.make_async_remote_copy(
        src_ref=src, dst_ref=dst, send_sem=send, recv_sem=recv, device_id=where, device_id_type=MESH
    )


def rms(values):
    factor = lax.rsqrt(jnp.mean(values * values, axis=-1, keepdims=True) + epsilon)
    return values * factor, factor


def kernel(
    n_pipe, n_dp, n_tensor,
    slot_ref, out_in, grad_in, host_in, gain_ref, up_in, down_in,
    nf_out, nb_out, th_out, gg_out,
    up, down, both, chosen, fwd_own, sav_own, hat_own,
    norm_f, norm_s, inc, part_f, part_b, sum_f, sum_b, end_f, end_b,
    mid, pair, gain_own, gain_dp, gain_mid, gain_tp,
    local_sem, z_send, z_recv, ag_send, ag_recv, rs_send, rs_recv, pr_send, pr_recv, gd_send, gd_recv, gt_send, gt_recv,
):
    s, d, t = lax.axis_index("pipe"), lax.axis_index("dp"), lax.axis_index("tensor")
    rows = out_in.shape[1] // n_tensor
    width, hidden_units = up.shape
    core = t % 2
    sibling = t + 1 - 2 * core
    across = [(t + 2 * p) % n_tensor for p in range(1, n_tensor // 2)]
    peers = [(t + p) % n_tensor for p in range(1, n_tensor)]
    dp_peers = [(d + p) % n_dp for p in range(1, n_dp)]
    after, before = (s + 1) % n_pipe, (s + n_pipe - 1) % n_pipe
    mirror, keeper = n_pipe - 1 - s, (2 * n_pipe - 2 - s) % n_pipe
    own = pl.ds(pl.multiple_of(t * rows, rows), rows)

    def chunk(ref, k):
        return ref.at[0, pl.ds(pl.multiple_of(k * rows, rows), rows)]

    barrier = pltpu.get_barrier_semaphore()
    @pl.when(keeper != s)
    def _():
        pl.semaphore_signal(barrier, inc=1, device_id={"pipe": keeper}, device_id_type=MESH)

    for where in [{"pipe": after}, {"pipe": before}, {"pipe": mirror}]:
        pl.semaphore_signal(barrier, inc=1, device_id=where, device_id_type=MESH)

    for k in dp_peers:
        pl.semaphore_signal(barrier, inc=1, device_id={"dp": k}, device_id_type=MESH)
    for k in peers:
        pl.semaphore_signal(barrier, inc=1, device_id={"tensor": k}, device_id_type=MESH)

    load_host = pltpu.make_async_copy(host_in.at[0, :, own], both, local_sem.at[0])
    load_host.start()
    load_up = pltpu.make_async_copy(up_in.at[0], up, local_sem.at[1])
    load_up.start()
    load_down = pltpu.make_async_copy(down_in.at[0], down, local_sem.at[2])
    load_down.start()
    load_host.wait()
    chosen[...] = both[slot_ref[0]]
    pl.semaphore_wait(barrier, 3 + len(dp_peers) + len(peers) + jnp.where(keeper != s, 1, 0))

    z_s = remote(chosen, sav_own, z_send.at[0], z_recv.at[0], pipe=mirror)
    z_g = remote(grad_in.at[0, own], inc.at[t], z_send.at[1], z_recv.at[1], pipe=before)
    z_f = remote(out_in.at[0, own], fwd_own, z_send.at[2], z_recv.at[2], pipe=after)
    z_t = remote(out_in.at[0, own], chunk(th_out, t), z_send.at[3], z_recv.at[3], pipe=keeper)
    l_t = pltpu.make_async_copy(out_in.at[0, own], chunk(th_out, t), local_sem.at[3])
    z_s.start()
    z_g.start()
    z_f.start()

    def gather_start(which, at):
        for i, k in enumerate([sibling] + across):
            remote(at(t), at(t), ag_send.at[which, i], ag_recv.at[which, t], tensor=k).start()

    def gather_pass(which, at):
        for i, k in enumerate(across):
            remote(at(k), at(k), ag_send.at[which, 4 + i], ag_recv.at[which, k], tensor=k).wait_recv()
            remote(at(k), at(k), ag_send.at[which, 4 + i], ag_recv.at[which, k], tensor=sibling).start()

    def gather_wait(which, at):
        for k in [sibling] + [k + 1 - 2 * core for k in across]:
            remote(at(k), at(k), ag_send.at[which, 0], ag_recv.at[which, k], tensor=sibling).wait_recv()

    def gather_sent(which, at):
        for i, k in enumerate([sibling] + across):
            remote(at(t), at(t), ag_send.at[which, i], ag_recv.at[which, t], tensor=k).wait_send()
        for i, k in enumerate(across):
            remote(at(k), at(k), ag_send.at[which, 4 + i], ag_recv.at[which, k], tensor=sibling).wait_send()

    at_s, at_g, at_f = (lambda k: norm_s.at[k]), (lambda k: inc.at[k]), (lambda k: norm_f.at[k])
    at_t, at_nb, at_nf = (
        functools.partial(chunk, th_out), functools.partial(chunk, nb_out), functools.partial(chunk, nf_out)
    )
    gains = gain_ref[...]

    z_s.wait_recv()
    hat, saved_factor = rms(sav_own[...].astype(F32))
    hat_own[...] = hat
    norm_s[t] = (hat * gains).astype(BF16)
    gather_start(0, at_s)
    z_g.wait_recv()
    gather_start(1, at_g)
    z_f.wait_recv()
    norm_f[t] = (rms(fwd_own[...].astype(F32))[0] * gains).astype(BF16)
    gather_start(2, at_f)

    @pl.when(keeper != s)
    def _():
        z_t.start()

    @pl.when(keeper == s)
    def _():
        l_t.start()

    gather_pass(0, at_s)
    gather_pass(1, at_g)
    gather_pass(2, at_f)
    gather_wait(0, at_s)
    gather_wait(1, at_g)

    tokens = n_tensor * rows
    nt = (((1,), (1,)), ((), ()))

    def cut(i):
        return pl.ds(pl.multiple_of(i * TILE, TILE), TILE)

    load_up.wait()
    load_down.wait()

    @pl.loop(0, hidden_units // TILE)
    def _(i):
        pre = jnp.dot(norm_s[...].reshape(tokens, width), up[:, cut(i)], preferred_element_type=F32)
        back = lax.dot_general(inc[...].reshape(tokens, width), down[cut(i), :], nt, preferred_element_type=F32)
        sigma = jax.nn.sigmoid(pre)
        mid[0, :, cut(i)] = (back * (sigma * (1.0 + pre * (1.0 - sigma)))).astype(BF16)

    @pl.loop(0, width // TILE)
    def _(i):
        part = lax.dot_general(mid[0], up[cut(i), :], nt, preferred_element_type=F32)
        part_b[:, :, cut(i)] = part.astype(BF16).reshape(n_tensor, rows, TILE)

    y_own, y_all = t // 2, n_tensor // 2
    far = [(y_own + p) % y_all for p in sorted(range(1, y_all), key=lambda p: -min(p, y_all - p))]

    def pair_copy(which, part, y):
        k = 2 * y + 1 - core
        return remote(part.at[k], pair.at[which, y], pr_send.at[which, y], pr_recv.at[which, y], tensor=sibling)

    def pair_sum(which, part, y):
        pair_copy(which, part, y).wait_recv()
        return part[2 * y + core].astype(F32) + pair[which, y].astype(F32)

    def scatter_start(which, part, total):
        for y in far + [y_own]:
            pair_copy(which, part, y).start()
        for i, y in enumerate(far):
            k = 2 * y + core
            part[k] = pair_sum(which, part, y).astype(BF16)
            remote(part.at[k], total.at[y_own], rs_send.at[which, i], rs_recv.at[which, y_own], tensor=k).start()

    def scatter_sum(which, part, total):
        acc = pair_sum(which, part, y_own)
        for i, y in enumerate(far):
            k = 2 * y + core
            remote(part.at[k], total.at[y], rs_send.at[which, i], rs_recv.at[which, y], tensor=k).wait_recv()
            acc += total[y].astype(F32)
        return acc

    def scatter_sent(which, part, total):
        for y in far + [y_own]:
            pair_copy(which, part, y).wait_send()
        for i, y in enumerate(far):
            k = 2 * y + core
            remote(part.at[k], total.at[y_own], rs_send.at[which, i], rs_recv.at[which, y_own], tensor=k).wait_send()

    scatter_start(0, part_b, sum_b)
    gather_wait(2, at_f)

    @pl.loop(0, hidden_units // TILE)
    def _(i):
        pre = jnp.dot(norm_f[...].reshape(tokens, width), up[:, cut(i)], preferred_element_type=F32)
        mid[1, :, cut(i)] = jax.nn.silu(pre).astype(BF16)

    @pl.loop(0, width // TILE)
    def _(i):
        part = jnp.dot(mid[1], down[:, cut(i)], preferred_element_type=F32)
        part_f[:, :, cut(i)] = part.astype(BF16).reshape(n_tensor, rows, TILE)

    scatter_start(1, part_f, sum_f)

    normed_grad = scatter_sum(0, part_b, sum_b)
    hat = hat_own[...]
    gain_own[...] = jnp.sum(normed_grad * hat, axis=0, keepdims=True)
    for i, k in enumerate(dp_peers):
        remote(gain_own, gain_dp.at[d], gd_send.at[i], gd_recv.at[d], dp=k).start()
    hat_grad = normed_grad * gains
    input_grad = saved_factor * (hat_grad - hat * jnp.mean(hat_grad * hat, axis=-1, keepdims=True))
    end_b[...] = (inc[t].astype(F32) + input_grad).astype(BF16)

    def ends_start(which, end, at):
        keep = pltpu.make_async_copy(end, at(t), local_sem.at[which])
        keep.start()
        for i, k in enumerate([sibling] + across):
            remote(end, at(t), ag_send.at[which, i], ag_recv.at[which, t], tensor=k).start()
        return keep

    keep_b = ends_start(4, end_b, at_nb)
    mixed = scatter_sum(1, part_f, sum_f)
    end_f[...] = (fwd_own[...].astype(F32) + mixed).astype(BF16)
    keep_f = ends_start(5, end_f, at_nf)

    @pl.when(keeper != s)
    def _():
        z_t.wait()

    @pl.when(keeper == s)
    def _():
        l_t.wait()

    gather_start(3, at_t)

    acc = gain_own[...]
    for i, k in enumerate(dp_peers):
        remote(gain_own, gain_dp.at[k], gd_send.at[i], gd_recv.at[k], dp=k).wait_recv()
        acc += gain_dp[k]
    gain_mid[...] = acc
    for i, k in enumerate(peers):
        remote(gain_mid, gain_tp.at[t], gt_send.at[i], gt_recv.at[t], tensor=k).start()

    gather_pass(4, at_nb)
    gather_pass(5, at_nf)
    gather_pass(3, at_t)

    for i, k in enumerate(peers):
        remote(gain_mid, gain_tp.at[k], gt_send.at[i], gt_recv.at[k], tensor=k).wait_recv()
        acc += gain_tp[k]
    gg_out[...] = acc

    gather_wait(4, at_nb)
    gather_wait(5, at_nf)
    gather_wait(3, at_t)
    keep_b.wait()
    keep_f.wait()
    z_s.wait_send()
    z_g.wait_send()
    z_f.wait_send()
    for which, at in enumerate((at_s, at_g, at_f, at_t, at_nb, at_nf)):
        gather_sent(which, at)
    scatter_sent(0, part_b, sum_b)
    scatter_sent(1, part_f, sum_f)
    for i, k in enumerate(dp_peers):
        remote(gain_own, gain_dp.at[d], gd_send.at[i], gd_recv.at[d], dp=k).wait_send()
    for i, k in enumerate(peers):
        remote(gain_mid, gain_tp.at[t], gt_send.at[i], gt_recv.at[t], tensor=k).wait_send()


def move_out(*refs):
    sources, ends, (sems, gain_sem) = refs[:4], refs[4:8], refs[8:]
    copies = [pltpu.make_async_copy(sources[3], ends[3], gain_sem)]
    rows = sources[0].shape[1] // CUTS
    for i in range(3):
        for j in range(CUTS):
            part = pl.ds(j * rows, rows)
            copies.append(pltpu.make_async_copy(sources[i].at[0, part], ends[i].at[0, part], sems.at[i, j]))
    for copy in copies:
        copy.start()
    for copy in copies:
        copy.wait()


def body(section_out, section_grad, hosted, send_slot, gain, w_up, w_down):
    n_pipe, n_dp, n_tensor = (lax.axis_size(a) for a in ("pipe", "dp", "tensor"))
    _, tokens, width = section_out.shape
    units = w_up.shape[2]
    rows = tokens // n_tensor
    dma = pltpu.SemaphoreType.DMA
    whole = jax.ShapeDtypeStruct(section_out.shape, BF16)
    anywhere = pl.BlockSpec(memory_space=pl.ANY)
    in_vmem = pl.BlockSpec(memory_space=pltpu.VMEM)
    gathered = pltpu.VMEM((n_tensor, rows, width), BF16)
    row_block = pltpu.VMEM((rows, width), BF16)
    gain_row = pltpu.VMEM((1, width), F32)
    results = pl.pallas_call(
        functools.partial(kernel, n_pipe, n_dp, n_tensor),
        out_shape=(whole, whole, whole, jax.ShapeDtypeStruct((1, width), F32)),
        in_specs=[
            pl.BlockSpec(memory_space=pltpu.SMEM), anywhere, anywhere, anywhere, in_vmem, anywhere, anywhere,
        ],
        out_specs=(anywhere, anywhere, anywhere, in_vmem),
        scratch_shapes=[
            pltpu.VMEM((width, units), BF16), pltpu.VMEM((units, width), BF16),
            pltpu.VMEM((hosted.shape[1], rows, width), BF16), row_block, row_block, row_block,
            pltpu.VMEM((rows, width), F32),
            gathered, gathered, gathered, gathered, gathered, gathered, gathered, row_block, row_block,
            pltpu.VMEM((2, tokens, units), BF16), pltpu.VMEM((2, n_tensor // 2, rows, width), BF16),
            gain_row, pltpu.VMEM((n_dp, 1, width), F32), gain_row, pltpu.VMEM((n_tensor, 1, width), F32),
            dma((6,)), dma((4,)), dma((4,)), dma((6, n_tensor)), dma((6, n_tensor)),
            dma((2, n_tensor)), dma((2, n_tensor)), dma((2, n_tensor)), dma((2, n_tensor)), dma((n_dp,)), dma((n_dp,)), dma((n_tensor,)), dma((n_tensor,)),
        ],
        compiler_params=pltpu.CompilerParams(
            collective_id=0, has_side_effects=True, vmem_limit_bytes=52 * 2**20
        ),
    )(send_slot, section_out, section_grad, hosted, gain, w_up, w_down)
    return pl.pallas_call(
        move_out,
        out_shape=tuple(jax.ShapeDtypeStruct(r.shape, r.dtype) for r in results),
        in_specs=[anywhere] * 4,
        out_specs=(anywhere,) * 4,
        scratch_shapes=[dma((3, CUTS)), dma(())],
        compiler_params=pltpu.CompilerParams(vmem_limit_bytes=16 * 2**20),
    )(*results)


def solution(mesh):
    placed = (
        P("pipe", "dp", None),
        P("pipe", "dp", None),
        P("pipe", None, "dp", None),
        P("pipe"),
        P("pipe", None),
        P("pipe", None, "tensor"),
        P("pipe", "tensor", None),
    )
    return jax.shard_map(
        body,
        mesh=mesh,
        in_specs=placed,
        out_specs=(
            P("pipe", "dp", None),
            P("pipe", "dp", None),
            P("pipe", "dp", None),
            P("pipe", None),
        ),
        check_vma=False,
    )
```

```python
import functools

import jax
import jax.numpy as jnp
from jax import lax
from jax.experimental import pallas as pl
from jax.experimental.pallas import tpu as pltpu
from jax.sharding import PartitionSpec as P

epsilon = 1e-05
MESH = pl.DeviceIdType.MESH
F32, BF16 = jnp.float32, jnp.bfloat16
UP_TILE, WIDE_TILE = 384, 512
CUTS = 4


def remote(src, dst, send, recv, **where):
    return pltpu.make_async_remote_copy(
        src_ref=src, dst_ref=dst, send_sem=send, recv_sem=recv, device_id=where, device_id_type=MESH
    )


def rms(values):
    factor = lax.rsqrt(jnp.mean(values * values, axis=-1, keepdims=True) + epsilon)
    return values * factor, factor


def kernel(
    n_pipe, n_dp, n_tensor,
    slot_ref, out_in, grad_in, host_in, gain_ref, up_in, down_in,
    nf_out, nb_out, th_out, gg_out,
    up, down, both, chosen, fwd_own, sav_own, hat_own,
    norm_f, norm_s, inc, part_f, part_b, sum_f, sum_b, end_f, end_b,
    mid, pair, gain_own, gain_dp, gain_mid, gain_tp,
    local_sem, z_send, z_recv, ag_send, ag_recv, rs_send, rs_recv, pr_send, pr_recv, gd_send, gd_recv, gt_send, gt_recv,
):
    s, d, t = lax.axis_index("pipe"), lax.axis_index("dp"), lax.axis_index("tensor")
    rows = out_in.shape[1] // n_tensor
    width, hidden_units = up.shape
    core = t % 2
    sibling = t + 1 - 2 * core
    steps = sorted(range(1, n_tensor // 2), key=lambda p: min(p, n_tensor // 2 - p))
    across = [(t + 2 * p) % n_tensor for p in steps]
    peers = [(t + p) % n_tensor for p in range(1, n_tensor)]
    dp_peers = [(d + p) % n_dp for p in range(1, n_dp)]
    after, before = (s + 1) % n_pipe, (s + n_pipe - 1) % n_pipe
    mirror, keeper = n_pipe - 1 - s, (2 * n_pipe - 2 - s) % n_pipe
    own = pl.ds(pl.multiple_of(t * rows, rows), rows)

    def chunk(ref, k):
        return ref.at[0, pl.ds(pl.multiple_of(k * rows, rows), rows)]

    barrier = pltpu.get_barrier_semaphore()
    @pl.when(keeper != s)
    def _():
        pl.semaphore_signal(barrier, inc=1, device_id={"pipe": keeper}, device_id_type=MESH)

    for where in [{"pipe": after}, {"pipe": before}, {"pipe": mirror}]:
        pl.semaphore_signal(barrier, inc=1, device_id=where, device_id_type=MESH)

    for k in dp_peers:
        pl.semaphore_signal(barrier, inc=1, device_id={"dp": k}, device_id_type=MESH)
    for k in peers:
        pl.semaphore_signal(barrier, inc=1, device_id={"tensor": k}, device_id_type=MESH)

    load_host = pltpu.make_async_copy(host_in.at[0, :, own], both, local_sem.at[0])
    load_host.start()
    load_up = pltpu.make_async_copy(up_in.at[0], up, local_sem.at[1])
    load_up.start()
    load_down = pltpu.make_async_copy(down_in.at[0], down, local_sem.at[2])
    load_down.start()
    load_host.wait()
    chosen[...] = both[slot_ref[0]]
    pl.semaphore_wait(barrier, 3 + len(dp_peers) + len(peers) + jnp.where(keeper != s, 1, 0))

    z_s = remote(chosen, sav_own, z_send.at[0], z_recv.at[0], pipe=mirror)
    z_g = remote(grad_in.at[0, own], inc.at[t], z_send.at[1], z_recv.at[1], pipe=before)
    z_f = remote(out_in.at[0, own], fwd_own, z_send.at[2], z_recv.at[2], pipe=after)
    z_t = remote(out_in.at[0, own], chunk(th_out, t), z_send.at[3], z_recv.at[3], pipe=keeper)
    l_t = pltpu.make_async_copy(out_in.at[0, own], chunk(th_out, t), local_sem.at[3])
    z_s.start()
    z_g.start()
    z_f.start()

    def gather_start(which, at):
        for i, k in enumerate(across[::-1] + [sibling]):
            remote(at(t), at(t), ag_send.at[which, i], ag_recv.at[which, t], tensor=k).start()

    def gather_pass(which, at):
        for i, k in enumerate(across):
            remote(at(k), at(k), ag_send.at[which, 4 + i], ag_recv.at[which, k], tensor=k).wait_recv()
            remote(at(k), at(k), ag_send.at[which, 4 + i], ag_recv.at[which, k], tensor=sibling).start()

    def gather_wait(which, at):
        for k in [sibling] + [k + 1 - 2 * core for k in across]:
            remote(at(k), at(k), ag_send.at[which, 0], ag_recv.at[which, k], tensor=sibling).wait_recv()

    def gather_sent(which, at):
        for i, k in enumerate(across[::-1] + [sibling]):
            remote(at(t), at(t), ag_send.at[which, i], ag_recv.at[which, t], tensor=k).wait_send()
        for i, k in enumerate(across):
            remote(at(k), at(k), ag_send.at[which, 4 + i], ag_recv.at[which, k], tensor=sibling).wait_send()

    at_s, at_g, at_f = (lambda k: norm_s.at[k]), (lambda k: inc.at[k]), (lambda k: norm_f.at[k])
    at_t, at_nb, at_nf = (
        functools.partial(chunk, th_out), functools.partial(chunk, nb_out), functools.partial(chunk, nf_out)
    )
    gains = gain_ref[...]

    z_s.wait_recv()
    hat, saved_factor = rms(sav_own[...].astype(F32))
    hat_own[...] = hat
    norm_s[t] = (hat * gains).astype(BF16)
    gather_start(0, at_s)
    z_g.wait_recv()
    gather_start(1, at_g)
    z_f.wait_recv()
    norm_f[t] = (rms(fwd_own[...].astype(F32))[0] * gains).astype(BF16)
    gather_start(2, at_f)

    gather_pass(0, at_s)
    gather_pass(1, at_g)
    gather_pass(2, at_f)

    @pl.when(keeper != s)
    def _():
        z_t.start()

    @pl.when(keeper == s)
    def _():
        l_t.start()

    gather_wait(0, at_s)
    gather_wait(1, at_g)

    tokens = n_tensor * rows
    nt = (((1,), (1,)), ((), ()))

    def cut(i, tile=UP_TILE):
        return pl.ds(pl.multiple_of(i * tile, tile), tile)

    load_up.wait()
    load_down.wait()

    @pl.loop(0, hidden_units // UP_TILE)
    def _(i):
        pre = jnp.dot(norm_s[...].reshape(tokens, width), up[:, cut(i)], preferred_element_type=F32)
        back = lax.dot_general(inc[...].reshape(tokens, width), down[cut(i), :], nt, preferred_element_type=F32)
        sigma = jax.nn.sigmoid(pre)
        mid[0, :, cut(i)] = (back * (sigma * (1.0 + pre * (1.0 - sigma)))).astype(BF16)

    @pl.loop(0, width // WIDE_TILE)
    def _(i):
        part = lax.dot_general(mid[0], up[cut(i, WIDE_TILE), :], nt, preferred_element_type=F32)
        part_b[:, :, cut(i, WIDE_TILE)] = part.astype(BF16).reshape(n_tensor, rows, WIDE_TILE)

    y_own, y_all = t // 2, n_tensor // 2
    far = [(y_own + p) % y_all for p in sorted(range(1, y_all), key=lambda p: -min(p, y_all - p))]

    def pair_copy(which, part, y):
        k = 2 * y + 1 - core
        return remote(part.at[k], pair.at[which, y], pr_send.at[which, y], pr_recv.at[which, y], tensor=sibling)

    def pair_sum(which, part, y):
        pair_copy(which, part, y).wait_recv()
        return part[2 * y + core].astype(F32) + pair[which, y].astype(F32)

    def scatter_start(which, part, total):
        for y in far + [y_own]:
            pair_copy(which, part, y).start()
        for i, y in enumerate(far):
            k = 2 * y + core
            part[k] = pair_sum(which, part, y).astype(BF16)
            remote(part.at[k], total.at[y_own], rs_send.at[which, i], rs_recv.at[which, y_own], tensor=k).start()

    def scatter_sum(which, part, total):
        acc = pair_sum(which, part, y_own)
        for i, y in enumerate(far):
            k = 2 * y + core
            remote(part.at[k], total.at[y], rs_send.at[which, i], rs_recv.at[which, y], tensor=k).wait_recv()
            acc += total[y].astype(F32)
        return acc

    def scatter_sent(which, part, total):
        for y in far + [y_own]:
            pair_copy(which, part, y).wait_send()
        for i, y in enumerate(far):
            k = 2 * y + core
            remote(part.at[k], total.at[y_own], rs_send.at[which, i], rs_recv.at[which, y_own], tensor=k).wait_send()

    scatter_start(0, part_b, sum_b)
    gather_wait(2, at_f)

    @pl.loop(0, hidden_units // UP_TILE)
    def _(i):
        pre = jnp.dot(norm_f[...].reshape(tokens, width), up[:, cut(i)], preferred_element_type=F32)
        mid[1, :, cut(i)] = jax.nn.silu(pre).astype(BF16)

    @pl.loop(0, width // WIDE_TILE)
    def _(i):
        part = jnp.dot(mid[1], down[:, cut(i, WIDE_TILE)], preferred_element_type=F32)
        part_f[:, :, cut(i, WIDE_TILE)] = part.astype(BF16).reshape(n_tensor, rows, WIDE_TILE)

    scatter_start(1, part_f, sum_f)

    normed_grad = scatter_sum(0, part_b, sum_b)
    hat = hat_own[...]
    gain_own[...] = jnp.sum(normed_grad * hat, axis=0, keepdims=True)
    for i, k in enumerate(dp_peers):
        remote(gain_own, gain_dp.at[d], gd_send.at[i], gd_recv.at[d], dp=k).start()
    hat_grad = normed_grad * gains
    input_grad = saved_factor * (hat_grad - hat * jnp.mean(hat_grad * hat, axis=-1, keepdims=True))
    end_b[...] = (inc[t].astype(F32) + input_grad).astype(BF16)

    def ends_start(which, end, at):
        keep = pltpu.make_async_copy(end, at(t), local_sem.at[which])
        keep.start()
        for i, k in enumerate(across[::-1] + [sibling]):
            remote(end, at(t), ag_send.at[which, i], ag_recv.at[which, t], tensor=k).start()
        return keep

    keep_b = ends_start(4, end_b, at_nb)
    mixed = scatter_sum(1, part_f, sum_f)
    end_f[...] = (fwd_own[...].astype(F32) + mixed).astype(BF16)
    keep_f = ends_start(5, end_f, at_nf)

    @pl.when(keeper != s)
    def _():
        z_t.wait()

    @pl.when(keeper == s)
    def _():
        l_t.wait()

    gather_start(3, at_t)

    acc = gain_own[...]
    for i, k in enumerate(dp_peers):
        remote(gain_own, gain_dp.at[k], gd_send.at[i], gd_recv.at[k], dp=k).wait_recv()
        acc += gain_dp[k]
    gain_mid[...] = acc
    for i, k in enumerate(peers):
        remote(gain_mid, gain_tp.at[t], gt_send.at[i], gt_recv.at[t], tensor=k).start()

    gather_pass(4, at_nb)
    gather_pass(5, at_nf)
    gather_pass(3, at_t)

    for i, k in enumerate(peers):
        remote(gain_mid, gain_tp.at[k], gt_send.at[i], gt_recv.at[k], tensor=k).wait_recv()
        acc += gain_tp[k]
    gg_out[...] = acc

    gather_wait(4, at_nb)
    gather_wait(5, at_nf)
    gather_wait(3, at_t)
    keep_b.wait()
    keep_f.wait()
    z_s.wait_send()
    z_g.wait_send()
    z_f.wait_send()
    for which, at in enumerate((at_s, at_g, at_f, at_t, at_nb, at_nf)):
        gather_sent(which, at)
    scatter_sent(0, part_b, sum_b)
    scatter_sent(1, part_f, sum_f)
    for i, k in enumerate(dp_peers):
        remote(gain_own, gain_dp.at[d], gd_send.at[i], gd_recv.at[d], dp=k).wait_send()
    for i, k in enumerate(peers):
        remote(gain_mid, gain_tp.at[t], gt_send.at[i], gt_recv.at[t], tensor=k).wait_send()


def move_out(*refs):
    sources, ends, (sems, gain_sem) = refs[:4], refs[4:8], refs[8:]
    copies = [pltpu.make_async_copy(sources[3], ends[3], gain_sem)]
    rows = sources[0].shape[1] // CUTS
    for i in range(3):
        for j in range(CUTS):
            part = pl.ds(j * rows, rows)
            copies.append(pltpu.make_async_copy(sources[i].at[0, part], ends[i].at[0, part], sems.at[i, j]))
    for copy in copies:
        copy.start()
    for copy in copies:
        copy.wait()


def body(section_out, section_grad, hosted, send_slot, gain, w_up, w_down):
    n_pipe, n_dp, n_tensor = (lax.axis_size(a) for a in ("pipe", "dp", "tensor"))
    _, tokens, width = section_out.shape
    units = w_up.shape[2]
    rows = tokens // n_tensor
    dma = pltpu.SemaphoreType.DMA
    whole = jax.ShapeDtypeStruct(section_out.shape, BF16)
    anywhere = pl.BlockSpec(memory_space=pl.ANY)
    in_vmem = pl.BlockSpec(memory_space=pltpu.VMEM)
    gathered = pltpu.VMEM((n_tensor, rows, width), BF16)
    row_block = pltpu.VMEM((rows, width), BF16)
    gain_row = pltpu.VMEM((1, width), F32)
    results = pl.pallas_call(
        functools.partial(kernel, n_pipe, n_dp, n_tensor),
        out_shape=(whole, whole, whole, jax.ShapeDtypeStruct((1, width), F32)),
        in_specs=[
            pl.BlockSpec(memory_space=pltpu.SMEM), anywhere, anywhere, anywhere, in_vmem, anywhere, anywhere,
        ],
        out_specs=(anywhere, anywhere, anywhere, in_vmem),
        scratch_shapes=[
            pltpu.VMEM((width, units), BF16), pltpu.VMEM((units, width), BF16),
            pltpu.VMEM((hosted.shape[1], rows, width), BF16), row_block, row_block, row_block,
            pltpu.VMEM((rows, width), F32),
            gathered, gathered, gathered, gathered, gathered, gathered, gathered, row_block, row_block,
            pltpu.VMEM((2, tokens, units), BF16), pltpu.VMEM((2, n_tensor // 2, rows, width), BF16),
            gain_row, pltpu.VMEM((n_dp, 1, width), F32), gain_row, pltpu.VMEM((n_tensor, 1, width), F32),
            dma((6,)), dma((4,)), dma((4,)), dma((6, n_tensor)), dma((6, n_tensor)),
            dma((2, n_tensor)), dma((2, n_tensor)), dma((2, n_tensor)), dma((2, n_tensor)), dma((n_dp,)), dma((n_dp,)), dma((n_tensor,)), dma((n_tensor,)),
        ],
        compiler_params=pltpu.CompilerParams(
            collective_id=0, has_side_effects=True, vmem_limit_bytes=52 * 2**20
        ),
    )(send_slot, section_out, section_grad, hosted, gain, w_up, w_down)
    return pl.pallas_call(
        move_out,
        out_shape=tuple(jax.ShapeDtypeStruct(r.shape, r.dtype) for r in results),
        in_specs=[anywhere] * 4,
        out_specs=(anywhere,) * 4,
        scratch_shapes=[dma((3, CUTS)), dma(())],
        compiler_params=pltpu.CompilerParams(vmem_limit_bytes=16 * 2**20),
    )(*results)


def solution(mesh):
    placed = (
        P("pipe", "dp", None),
        P("pipe", "dp", None),
        P("pipe", None, "dp", None),
        P("pipe"),
        P("pipe", None),
        P("pipe", None, "tensor"),
        P("pipe", "tensor", None),
    )
    return jax.shard_map(
        body,
        mesh=mesh,
        in_specs=placed,
        out_specs=(
            P("pipe", "dp", None),
            P("pipe", "dp", None),
            P("pipe", "dp", None),
            P("pipe", None),
        ),
        check_vma=False,
    )
```
